256 devices in a mesh: doc: 8 (over x, core), term: 32 (over y, z).
Axes of the slice: x: 4, y: 4, z: 8, core: 2. Of those that a mesh axis runs over, the one named last changes fastest.
Arguments:
- counts: int32 [3072, 262144], P('doc', 'term'), may hold values from 0 to 7
- doc_freq: int32 [262144], P('term'), may hold values from 1 to 2097151, as said below
- sketch_seed: int32 [1], replicated, may hold values from 0 to 1048575
Outputs:
- ortho_basis: float32 [3072, 256], P('doc')
- projected_panel: bfloat16 [256, 262144], P('doc', 'term')
- column_mean: float32 [262144], P('term')
The draws below stay inside these ranges and needn't reach their ends.
Inputs may be any that keep to these rules, and one draw needn't show every extreme that they name: `doc_freq`: document frequencies spread evenly in their logarithm.
All inputs are finite; a program needn't handle non-finite values.
Results may differ from the reference program's by a relative error of at most 0.018.
Values may be sent and summed in bfloat16 or wider, within the bound.
No kernel may reach another device: no remote copies, remote signals or barrier semaphores. Data moves between devices by JAX's collectives and lax.ppermute only.
A program may use at most 64 MiB of HBM per device.

```python
import jax
import jax.numpy as jnp
from jax import lax

TERMS = 262144
SKETCH = 256
CORPUS = 2000000000
DOC_DEV = 384
DOCS = 3072
N_DOC = 8
N_TERM = 32


def draw_doc_freq(key, part):
    key = jax.random.fold_in(key, 7)
    exp_key, low_key, spot_key = jax.random.split(key, 3)
    exponent = jax.random.randint(exp_key, (TERMS,), 0, 21, dtype=jnp.int32)
    base_value = jnp.left_shift(jnp.int32(1), exponent)
    remainder = jax.random.randint(low_key, (TERMS,), 0, 2097152, dtype=jnp.int32)
    values = base_value + remainder % base_value
    spots = jax.random.permutation(spot_key, TERMS)[:2].astype(jnp.int32)
    values = values.at[spots[0]].set(jnp.int32(2097151))
    values = values.at[spots[1]].set(jnp.int32(1))
    return values


def touch_ends(values, stream_key, low, largest):
    longest = values.shape.index(max(values.shape))
    spots = []
    for shift in (0, 1):
        where = [jax.random.randint(jax.random.fold_in(stream_key, axis), (), 0, length) for axis, length in enumerate(values.shape)]
        where[longest] = (where[longest] + shift) % values.shape[longest]
        spots.append(tuple(where))
    return values.at[spots[0]].set(low).at[spots[1]].set(largest)


def setup_inputs(seed: int = 0) -> dict:
    key_of = jax.random.split(jax.random.key(seed), 4)
    return {
        "counts": touch_ends(jax.random.randint(key_of[0], (DOCS, TERMS), 0, 8), jax.random.fold_in(key_of[0], 1), 0, 7).astype(jnp.int32),
        "doc_freq": draw_doc_freq(jax.random.fold_in(key_of[3], 71), 0),
        "sketch_seed": jax.random.randint(key_of[2], (1,), 0, 1048576).astype(jnp.int32),
    }


byte_sum_std = 147.8

def sketch_tile(seed_value, first_term, row_count, col_count):
    term_ids = first_term + lax.iota(jnp.int32, row_count)
    columns = lax.iota(jnp.int32, col_count)
    hashed = term_ids[:, None] * col_count + columns[None, :]
    hashed = hashed ^ seed_value * 668265263
    hashed = hashed * 1640531527
    hashed = hashed ^ lax.shift_right_logical(hashed, jnp.int32(15))
    hashed = hashed * 739982445
    hashed = hashed ^ lax.shift_right_logical(hashed, jnp.int32(13))
    summed = (hashed & 255) + (lax.shift_right_logical(hashed, jnp.int32(8)) & 255)
    summed = summed + (lax.shift_right_logical(hashed, jnp.int32(16)) & 255)
    summed = summed + (lax.shift_right_logical(hashed, jnp.int32(24)) & 255)
    factor = 1.0 / (byte_sum_std * TERMS ** 0.5)
    return ((summed - 510).astype(jnp.float32) * factor).astype(jnp.bfloat16)

def tfidf_tile(counts_tile, df_tile):
    counted = jnp.maximum(counts_tile.astype(jnp.float32), 1.0)
    term_freq = jnp.where(counts_tile > 0, 1.0 + jnp.log(counted), 0.0)
    inverse = 1.0 + jnp.log(jnp.float32(CORPUS) / df_tile.astype(jnp.float32))
    return term_freq * inverse[None, :]

def center_tile(tfidf, column_mean):
    return (tfidf - column_mean[None, :]).astype(jnp.bfloat16)

def reference(counts, doc_freq, sketch_seed):
    block_cols = TERMS // N_TERM
    seed_value = sketch_seed[0]
    block_ids = jnp.arange(N_TERM, dtype=jnp.int32)

    def weighted_block(block_index):
        first_term = (block_index * block_cols).astype(jnp.int32)
        counts_tile = lax.dynamic_slice_in_dim(counts, first_term, block_cols, 1)
        df_tile = lax.dynamic_slice_in_dim(doc_freq, first_term, block_cols, 0)
        tfidf = tfidf_tile(counts_tile, df_tile)
        column_mean = jnp.sum(tfidf, axis=0) / jnp.float32(DOCS)
        return (first_term, center_tile(tfidf, column_mean), column_mean)

    def sketch_step(running, block_index):
        first_term, weighted, _ = weighted_block(block_index)
        test_matrix = sketch_tile(seed_value, first_term, block_cols, SKETCH)
        product = jnp.dot(weighted.astype(jnp.float32), test_matrix.astype(jnp.float32), precision=lax.Precision.HIGHEST, preferred_element_type=jnp.float32)
        return (running + product, None)
    sketch, _ = lax.scan(sketch_step, jnp.zeros((DOCS, SKETCH), jnp.float32), block_ids)
    gram_matrix = jnp.dot(sketch.T.astype(jnp.float32), sketch.astype(jnp.float32), precision=lax.Precision.HIGHEST, preferred_element_type=jnp.float32)
    lower_factor = jnp.linalg.cholesky(gram_matrix)
    ortho_basis = lax.linalg.triangular_solve(lower_factor, sketch.T, left_side=True, lower=True).T
    basis_blocks = ortho_basis.astype(jnp.bfloat16).astype(jnp.float32).reshape(N_DOC, DOC_DEV, SKETCH)

    def panel_step(running, block_index):
        _, weighted, column_mean = weighted_block(block_index)
        weighted_blocks = weighted.astype(jnp.float32).reshape(N_DOC, DOC_DEV, block_cols)
        partials = jnp.einsum('dks,dkc->dsc', basis_blocks.astype(jnp.float32), weighted_blocks.astype(jnp.float32), precision=lax.Precision.HIGHEST, preferred_element_type=jnp.float32)
        rounded = lax.optimization_barrier(partials.astype(jnp.bfloat16))
        total = jnp.sum(rounded.astype(jnp.float32), axis=0)
        return (running, (total.astype(jnp.bfloat16), column_mean))
    _, (stacked, mean_blocks) = lax.scan(panel_step, jnp.zeros((), jnp.float32), block_ids)
    projected_panel = stacked.transpose(1, 0, 2).reshape(SKETCH, TERMS)
    column_mean = mean_blocks.reshape(TERMS)
    return (ortho_basis, projected_panel, column_mean)
```

```python
import math

import jax
import jax.numpy as jnp
import numpy as np
from jax import lax
from jax.experimental import pallas as pl
from jax.experimental.pallas import tpu as pltpu
from jax.sharding import Mesh
from jax.sharding import PartitionSpec as P

TERMS = 262144
SKETCH = 256
CORPUS = 2000000000
BYTE_SUM_STD = 147.8
FACTOR = 1.0 / (BYTE_SUM_STD * TERMS**0.5)
HIGHEST = lax.Precision.HIGHEST
F32, BF16, I32 = jnp.float32, jnp.bfloat16, jnp.int32
VMEM_LIMIT = 48 * 1024 * 1024
LANES = 128
PIVOTS = 16
TAIL = 16


def log_count(counts):
    return jnp.log(jnp.maximum(counts.astype(F32), math.exp(-1.0)))


def idf_of(doc_freq):
    return 1.0 + jnp.log(jnp.float32(CORPUS) / doc_freq.astype(F32))


def three_parts(value):
    high = value.astype(BF16)
    rest = value - high.astype(F32)
    middle = rest.astype(BF16)
    low = (rest - middle.astype(F32)).astype(BF16)
    return high, middle, low


def parts_tile(value, rows, shape):
    high, middle, low = (part.astype(F32) for part in three_parts(value))
    where = lax.broadcasted_iota(I32, shape, 0)
    tile = jnp.where(where == 0, high, jnp.where(where == 1, middle, jnp.where(where == 2, low, 0.0)))
    return tile.astype(BF16)


def sketch_kernel(scal_ref, counts_ref, df_ref, s_ref, w_ref, lsum_ref, acc, om):
    step, steps = pl.program_id(0), pl.num_programs(0)
    rows, cols = counts_ref.shape
    first = scal_ref[1] + step * cols
    key = scal_ref[0] * 668265263
    idf = idf_of(df_ref[...])

    @pl.when(step == 0)
    def _():
        acc[...] = jnp.zeros_like(acc)

    for tile in range(cols // LANES):
        at = slice(tile * LANES, (tile + 1) * LANES)
        logs = log_count(counts_ref[:, at])
        total = jnp.sum(logs, axis=0, keepdims=True)
        mean = total * (1.0 / rows)
        lsum_ref[tile : tile + 1, :] = total
        w_ref[:rows, at] = ((logs - mean) * idf[:, at]).astype(BF16)
        w_ref[rows:, at] = parts_tile(idf[:, at] * (1.0 + mean), TAIL, (TAIL, LANES))

    lane = lax.broadcasted_iota(I32, (1, LANES), 1)
    low_key, high_key = key & 255, key & -256
    group = 64
    local = lax.broadcasted_iota(I32, (group, LANES), 0)
    for g in range(cols // group):
        terms = (local + (first + g * group)) * SKETCH
        row_part = (terms ^ high_key) * 1640531527
        for half in range(SKETCH // LANES):
            col_part = ((lane + half * LANES) ^ low_key) * 1640531527
            h = row_part + col_part
            h = h ^ lax.shift_right_logical(h, jnp.int32(15))
            h = h * 739982445
            h = h ^ lax.shift_right_logical(h, jnp.int32(13))
            pair = (h & 0x00FF00FF) + (lax.shift_right_logical(h, jnp.int32(8)) & 0x00FF00FF)
            byte_sum = (pair & 0xFFFF) + lax.shift_right_logical(pair, jnp.int32(16))
            value = (byte_sum - 510).astype(F32) * FACTOR
            om[g * group : (g + 1) * group, half * LANES : (half + 1) * LANES] = value.astype(BF16)

    acc[...] += jnp.dot(w_ref[...], om[...], preferred_element_type=F32)

    @pl.when(step == steps - 1)
    def _():
        shift = jnp.sum(acc[rows:, :], axis=0, keepdims=True)
        for half in range(SKETCH // LANES):
            at = slice(half * LANES, (half + 1) * LANES)
            s_ref[half * rows : (half + 1) * rows, :] = acc[:rows, at] + shift[:, at]


def sketch_call(scalars, counts, doc_freq):
    rows, cols = counts.shape
    block = 1024
    return pl.pallas_call(
        sketch_kernel,
        grid=(cols // block,),
        in_specs=[
            pl.BlockSpec(memory_space=pltpu.SMEM),
            pl.BlockSpec((rows, block), lambda i: (0, i)),
            pl.BlockSpec((1, block), lambda i: (0, i)),
        ],
        out_specs=[
            pl.BlockSpec((2 * rows, LANES), lambda i: (0, 0)),
            pl.BlockSpec((rows + TAIL, block), lambda i: (0, i)),
            pl.BlockSpec((block // LANES, LANES), lambda i: (i, 0)),
        ],
        out_shape=[
            jax.ShapeDtypeStruct((2 * rows, LANES), F32),
            jax.ShapeDtypeStruct((rows + TAIL, cols), BF16),
            jax.ShapeDtypeStruct((cols // LANES, LANES), F32),
        ],
        scratch_shapes=[pltpu.VMEM((rows + TAIL, SKETCH), F32), pltpu.VMEM((block, SKETCH), BF16)],
        compiler_params=pltpu.CompilerParams(vmem_limit_bytes=VMEM_LIMIT),
        name="sketch",
    )(scalars, counts, doc_freq.reshape(1, cols))


def gram_kernel(scal_ref, g_ref, gram_ref, own_ref, full):
    parts, held, _ = g_ref.shape
    half_parts = parts // 2
    held -= TAIL
    docs = 4
    chunk = held // docs
    rows = chunk * half_parts
    for t in range(half_parts):
        for half in range(2):
            block = g_ref[t + half_parts * half].astype(F32)
            mean = block[held : held + 1] + block[held + 1 : held + 2] + block[held + 2 : held + 3]
            value = block[:held] + mean
            at = slice(half * LANES, (half + 1) * LANES)
            for x in range(docs):
                full[x * rows + chunk * t : x * rows + chunk * (t + 1), at] = value[chunk * x : chunk * (x + 1)]
    mean = jnp.sum(full[...], axis=0, keepdims=True) * (1.0 / (docs * rows))
    centred = full[...] - mean
    full[...] = centred
    gram_ref[:SKETCH, :] = lax.dot_general(
        centred, centred, (((0,), (0,)), ((), ())), precision=HIGHEST, preferred_element_type=F32
    )
    row = lax.broadcasted_iota(I32, (8, SKETCH), 0)
    gram_ref[SKETCH:, :] = jnp.where(row == 0, mean, 0.0)
    own_ref[...] = full[pl.ds(pl.multiple_of(scal_ref[0] * rows, 8), rows), :]


def gram_call(scalars, gathered, rows):
    return pl.pallas_call(
        gram_kernel,
        in_specs=[pl.BlockSpec(memory_space=pltpu.SMEM), pl.BlockSpec(memory_space=pltpu.VMEM)],
        out_specs=[pl.BlockSpec(memory_space=pltpu.VMEM)] * 2,
        out_shape=[
            jax.ShapeDtypeStruct((SKETCH + 8, SKETCH), F32),
            jax.ShapeDtypeStruct((rows, SKETCH), F32),
        ],
        scratch_shapes=[pltpu.VMEM((4 * rows, SKETCH), F32)],
        compiler_params=pltpu.CompilerParams(vmem_limit_bytes=VMEM_LIMIT),
        name="gram",
    )(scalars, gathered)


def basis_kernel(scal_ref, mine_ref, theirs_ref, own_ref, q_ref, bt_ref, work):
    my_x, my_core = scal_ref[0], scal_ref[1]
    size = SKETCH
    apart = mine_ref[size:, :] - theirs_ref[size:, :]
    docs = 4 * own_ref.shape[0]
    shift = lax.dot_general(apart, apart, (((0,), (0,)), ((), ())), precision=HIGHEST, preferred_element_type=F32)
    work[...] = (mine_ref[:size, :] + theirs_ref[:size, :]) + (0.5 * docs) * shift

    lane = lax.broadcasted_iota(I32, (PIVOTS, LANES), 1)
    sub = lax.broadcasted_iota(I32, (PIVOTS, LANES), 0)
    for block in range(size // PIVOTS):
        start = block * PIVOTS
        panel = work[start : start + PIVOTS, :]
        spread = [jnp.broadcast_to(panel[:, start + k : start + k + 1], (PIVOTS, LANES)) for k in range(PIVOTS)]
        halves = []
        for half in range(size // LANES):
            piece = panel[:, half * LANES : (half + 1) * LANES]
            local = lane - (start - half * LANES)
            if start // LANES == half:
                piece = jnp.where((local >= 0) & (local < PIVOTS), jnp.where(local == sub, 1.0, 0.0), piece)
            halves.append(piece)
        pivots = jnp.zeros((PIVOTS, LANES), F32)
        for j in range(PIVOTS):
            pivot = jnp.broadcast_to(spread[j][j : j + 1, :], (PIVOTS, LANES))
            pivots = jnp.where(sub == j, pivot, pivots)
            if j + 1 < PIVOTS:
                scale = jnp.where(sub > j, spread[j] * (1.0 / pivot), 0.0)
                for k in range(j + 1, PIVOTS):
                    spread[k] = spread[k] - scale * spread[k][j : j + 1, :]
                halves = [piece - scale * piece[j : j + 1, :] for piece in halves]
        root = lax.rsqrt(pivots)
        factor_rows = jnp.concatenate([piece * root for piece in halves], axis=1)
        work[start : start + PIVOTS, :] = factor_rows
        rest = start + PIVOTS
        if rest < size:
            update = lax.dot_general(
                factor_rows, factor_rows, (((0,), (0,)), ((), ())), precision=HIGHEST, preferred_element_type=F32
            )
            old = work[rest:, :]
            column = lax.broadcasted_iota(I32, old.shape, 1)
            old = jnp.where((column >= start) & (column < rest), 0.0, old)
            work[rest:, :] = old - update[rest:, :]

    row = lax.broadcasted_iota(I32, (size, size), 0)
    column = lax.broadcasted_iota(I32, (size, size), 1)
    inverse = jnp.where(column <= row, work[...], 0.0)
    own = own_ref[...] + 0.5 * apart[0:1, :]
    contract = (((1,), (1,)), ((), ()))
    q_ref[...] = lax.dot_general(own, inverse, contract, precision=HIGHEST, preferred_element_type=F32)
    flipped = lax.dot_general(inverse, own, contract, precision=HIGHEST, preferred_element_type=F32).astype(BF16)
    rows = size // 8
    for x in range(4):
        for core in range(2):
            piece = flipped[rows * (2 * x + core) : rows * (2 * x + core + 1)]
            bt_ref[(my_core + core) & 1, (x - my_x) & 3] = piece


def basis_call(scalars, mine, theirs, own):
    rows = own.shape[0]
    return pl.pallas_call(
        basis_kernel,
        in_specs=[pl.BlockSpec(memory_space=pltpu.SMEM)] + [pl.BlockSpec(memory_space=pltpu.VMEM)] * 3,
        out_specs=[pl.BlockSpec(memory_space=pltpu.VMEM)] * 2,
        out_shape=[
            jax.ShapeDtypeStruct((rows, SKETCH), F32),
            jax.ShapeDtypeStruct((2, 4, SKETCH // 8, rows), BF16),
        ],
        scratch_shapes=[pltpu.VMEM((SKETCH, SKETCH), F32)],
        compiler_params=pltpu.CompilerParams(vmem_limit_bytes=VMEM_LIMIT),
        name="basis",
    )(scalars, mine, theirs, own)


def project_kernel(bt_ref, w_ref, apart_ref, *out_refs):
    pieces, rows, depth = bt_ref.shape[1:]
    left = bt_ref[0].reshape(pieces * rows, depth)
    sums = jnp.sum(left.astype(F32), axis=1, keepdims=True)
    product = jnp.dot(left, w_ref[:depth, :], preferred_element_type=F32) + sums * apart_ref[...]
    product = product.astype(BF16)
    for k, out_ref in enumerate(out_refs):
        out_ref[...] = product[k * rows : (k + 1) * rows]


def project_call(basis, which, weighted, apart):
    _, pieces, rows, depth = basis.shape
    held, cols = weighted.shape
    block = 2048
    return pl.pallas_call(
        project_kernel,
        grid=(cols // block,),
        in_specs=[
            pl.BlockSpec((1, pieces, rows, depth), lambda i: (which, 0, 0, 0)),
            pl.BlockSpec((held, block), lambda i: (0, i)),
            pl.BlockSpec((1, block), lambda i: (0, i)),
        ],
        out_specs=[pl.BlockSpec((rows, block), lambda i: (0, i))] * pieces,
        out_shape=[jax.ShapeDtypeStruct((rows, cols), BF16)] * pieces,
        compiler_params=pltpu.CompilerParams(vmem_limit_bytes=VMEM_LIMIT),
        name="project",
    )(basis, weighted, apart)


def swap(value):
    return lax.ppermute(value, "core", [(0, 1), (1, 0)])


def shift_x(value, by):
    return lax.ppermute(value, "x", [(i, (i + by) % 4) for i in range(4)])


def body(counts, doc_freq, sketch_seed):
    rows, cols = counts.shape
    terms_axes = ("y", "z")
    parts = lax.axis_size(terms_axes)
    docs = lax.axis_size("x")
    my_x, my_core = lax.axis_index("x"), lax.axis_index("core")
    first_term = lax.axis_index(terms_axes) * cols
    scalars = jnp.stack([sketch_seed[0], first_term.astype(I32)])
    places = jnp.stack([my_x, my_core]).astype(I32)

    sketch_part, weighted, log_sums = sketch_call(scalars, counts, doc_freq)

    chunk = 2 * rows // parts
    pieces = lax.all_to_all(sketch_part.reshape(parts, chunk, LANES), terms_axes, 0, 0)
    share = jnp.sum(pieces, axis=0)
    block = jnp.concatenate([share, log_sums], axis=0)
    block = lax.all_to_all(jnp.broadcast_to(block[None], (docs,) + block.shape), "x", 0, 0)
    held = block[:, :chunk].reshape(docs * chunk, LANES)
    core_sums = jnp.sum(block[:, chunk:], axis=0)
    other_sums = swap(core_sums)

    centre = jnp.mean(held, axis=0, keepdims=True)
    sent = jnp.concatenate(
        [(held - centre).astype(BF16), *three_parts(centre), jnp.zeros((TAIL - 3, LANES), BF16)], axis=0
    )
    gathered = lax.all_to_all(jnp.broadcast_to(sent[None], (parts,) + sent.shape), terms_axes, 0, 0)
    mine, own = gram_call(places, gathered, rows)
    basis, flipped = basis_call(places, mine, swap(mine), own)

    log_mean = (core_sums + other_sums) * (1.0 / (rows * docs * lax.axis_size("core")))
    idf = idf_of(doc_freq)
    column_mean = idf * (1.0 + log_mean.reshape(cols))
    apart = idf * (log_sums * (1.0 / rows) - log_mean).reshape(cols)
    apart = apart.reshape(1, cols)

    theirs = project_call(flipped, 1, weighted, apart)
    theirs = [swap(piece) for piece in theirs]
    ours = project_call(flipped, 0, weighted, apart)
    sums = [(a.astype(F32) + b.astype(F32)).astype(BF16) for a, b in zip(ours, theirs)]
    total = sums[0].astype(F32)
    for by in (2, 1, 3):
        total = total + shift_x(sums[by], by).astype(F32)
    return (basis, total.astype(BF16), column_mean)


def solution(mesh):
    split = Mesh(np.array(mesh.devices).reshape(4, 2, 4, 8), ("x", "core", "y", "z"))
    docs, terms = ("x", "core"), ("y", "z")
    return jax.shard_map(
        body,
        mesh=split,
        in_specs=(P(docs, terms), P(terms), P()),
        out_specs=(P(docs, None), P(docs, terms), P(terms)),
        check_vma=False,
    )
```

```python
import functools
import math

import jax
import jax.numpy as jnp
import numpy as np
from jax import lax
from jax.experimental import pallas as pl
from jax.experimental.pallas import tpu as pltpu
from jax.sharding import Mesh
from jax.sharding import PartitionSpec as P

TERMS = 262144
SKETCH = 256
CORPUS = 2000000000
BYTE_SUM_STD = 147.8
FACTOR = 1.0 / (BYTE_SUM_STD * TERMS**0.5)
HIGHEST = lax.Precision.HIGHEST
F32, BF16, I32 = jnp.float32, jnp.bfloat16, jnp.int32
VMEM_LIMIT = 16 * 1024 * 1024
LANES = 128
PIVOTS = 32
TAIL = 16
MEAN_ROWS = 8
TRIANGLE = 192
MEANS = 16


def log_count(counts):
    return jnp.log(jnp.maximum(counts.astype(F32), math.exp(-1.0)))


def idf_of(doc_freq):
    return 1.0 + jnp.log(jnp.float32(CORPUS) / doc_freq.astype(F32))


def three_parts(value):
    high = value.astype(BF16)
    rest = value - high.astype(F32)
    middle = rest.astype(BF16)
    low = (rest - middle.astype(F32)).astype(BF16)
    return high, middle, low


def parts_tile(value, rows):
    high, middle, low = (part.astype(F32) for part in three_parts(value))
    where = lax.broadcasted_iota(I32, (rows, value.shape[1]), 0)
    tile = jnp.where(where == 0, high, jnp.where(where == 1, middle, jnp.where(where == 2, low, 0.0)))
    return tile.astype(BF16)


def sketch_kernel(
    seed_ref, counts_hbm, df_hbm, s_ref, w_hbm, lsum_ref, centre_ref, idf, counts, df, om, wb, in_sems, out_sems, df_sem
):
    rows, cols = counts_hbm.shape
    strip = rows // in_sems.shape[0]
    chunk = cols // out_sems.shape[0]

    def load(i):
        at = pl.ds(i * strip, strip)
        return pltpu.make_async_copy(counts_hbm.at[at], counts.at[at], in_sems.at[i])

    def store(i):
        at = pl.ds(pl.multiple_of(i * chunk, chunk), chunk)
        return pltpu.make_async_copy(wb.at[:, at], w_hbm.at[:, at], out_sems.at[i])

    load_df = pltpu.make_async_copy(df_hbm, df, df_sem)
    load_df.start()
    for i in range(rows // strip):
        load(i).start()

    first = lax.axis_index(("y", "z")) * (cols * SKETCH)
    key = seed_ref[0] * 668265263
    low_key, high_key = key & 255, key & -256
    lane = lax.broadcasted_iota(I32, (1, LANES), 1)
    col_parts = [((lane + half * LANES) ^ low_key) * 1640531527 for half in range(SKETCH // LANES)]
    group = 256
    local = lax.broadcasted_iota(I32, (group, LANES), 0) * SKETCH + first

    def hash_rows(g, carry):
        row_part = ((local + g * (group * SKETCH)) ^ high_key) * 1640531527
        for half, col_part in enumerate(col_parts):
            h = row_part + col_part
            h = h ^ lax.shift_right_logical(h, jnp.int32(15))
            h = h * 739982445
            h = h ^ lax.shift_right_logical(h, jnp.int32(13))
            pair = (h & 0x00FF00FF) + (lax.shift_right_logical(h, jnp.int32(8)) & 0x00FF00FF)
            byte_sum = lax.shift_right_logical(pair * 65537, jnp.int32(16))
            value = (byte_sum - 510).astype(F32).astype(BF16)
            om[pl.ds(pl.multiple_of(g * group, group), group), half * LANES : (half + 1) * LANES] = value
        return carry

    lax.fori_loop(0, cols // group, hash_rows, 0)

    load_df.wait()
    idf[...] = idf_of(df[...])
    for i in range(rows // strip):
        load(i).wait()

    strip_rows = 32

    def weigh(tile):
        at = pl.ds(pl.multiple_of(tile * LANES, LANES), LANES)
        part = log_count(counts[:strip_rows, at])
        centre = jnp.sum(part, axis=0, keepdims=True) * (1.0 / strip_rows)
        scale = idf[pl.ds(tile, 1), :]
        wb[:strip_rows, at] = ((part - centre) * scale).astype(BF16)
        wb[rows:, at] = parts_tile(scale * (1.0 + centre), TAIL)
        centre_ref[pl.ds(tile, 1), :] = centre
        for r in range(strip_rows, rows, strip_rows):
            values = log_count(counts[r : r + strip_rows, at])
            part = part + values
            wb[r : r + strip_rows, at] = ((values - centre) * scale).astype(BF16)
        lsum_ref[pl.ds(tile, 1), :] = jnp.sum(part, axis=0, keepdims=True)

    def weigh_chunk(i, carry):
        per_chunk = chunk // LANES

        def one(k, c):
            weigh(i * per_chunk + k)
            return c

        lax.fori_loop(0, per_chunk, one, 0, unroll=2)
        store(i).start()
        return carry

    lax.fori_loop(0, cols // chunk, weigh_chunk, 0)

    product = jnp.dot(wb[...], om[...], preferred_element_type=F32) * FACTOR
    centre = jnp.sum(product[rows:, :], axis=0, keepdims=True)
    shares = s_ref.shape[0] // 2
    share = rows // shares
    for half in range(SKETCH // LANES):
        at = slice(half * LANES, (half + 1) * LANES)
        tail = parts_tile(centre[:, at], MEAN_ROWS).astype(F32)
        for t in range(shares):
            value = jnp.concatenate([product[share * t : share * (t + 1), at], tail], axis=0)
            s_ref[shares * half + t] = value.astype(BF16)
    for i in range(cols // chunk):
        store(i).wait()


def sketch_call(seed, counts, doc_freq, parts):
    rows, cols = counts.shape
    in_vmem = pl.BlockSpec(memory_space=pltpu.VMEM)
    in_hbm = pl.BlockSpec(memory_space=pltpu.HBM)
    return pl.pallas_call(
        sketch_kernel,
        in_specs=[pl.BlockSpec(memory_space=pltpu.SMEM), in_hbm, in_hbm],
        out_specs=[in_vmem, in_hbm, in_vmem, in_vmem, in_vmem],
        out_shape=[
            pltpu.VMEM((parts, 2 * rows // parts + MEAN_ROWS, LANES), BF16),
            pltpu.HBM((rows + TAIL, cols), BF16),
        ]
        + [jax.ShapeDtypeStruct((cols // LANES, LANES), F32)] * 3,
        scratch_shapes=[
            pltpu.VMEM((rows, cols), I32),
            pltpu.VMEM((cols // LANES, LANES), I32),
            pltpu.VMEM((cols, SKETCH), BF16),
            pltpu.VMEM((rows + TAIL, cols), BF16),
            pltpu.SemaphoreType.DMA((8,)),
            pltpu.SemaphoreType.DMA((8,)),
            pltpu.SemaphoreType.DMA,
        ],
        compiler_params=pltpu.CompilerParams(vmem_limit_bytes=40 * 1024 * 1024),
        name="sketch",
    )(
        seed,
        pltpu.with_memory_space_constraint(counts, pltpu.HBM),
        pltpu.with_memory_space_constraint(doc_freq.reshape(cols // LANES, LANES), pltpu.HBM),
    )


def share_kernel(pieces_ref, out_ref):
    total = pieces_ref[0].astype(F32)
    for t in range(1, pieces_ref.shape[0]):
        total = total + pieces_ref[t].astype(F32)
    held = total.shape[0] - MEAN_ROWS
    centre = total[held : held + 1] + total[held + 1 : held + 2] + total[held + 2 : held + 3]
    value = jnp.concatenate([total[:held], parts_tile(centre, MEAN_ROWS).astype(F32)], axis=0).astype(BF16)
    for t in range(out_ref.shape[0]):
        out_ref[t] = value


def share_call(pieces):
    return pl.pallas_call(
        share_kernel,
        in_specs=[pl.BlockSpec(memory_space=pltpu.VMEM)],
        out_specs=pl.BlockSpec(memory_space=pltpu.VMEM),
        out_shape=pltpu.VMEM(pieces.shape, BF16),
        compiler_params=pltpu.CompilerParams(vmem_limit_bytes=VMEM_LIMIT),
        name="share",
    )(pieces)


def gram_kernel(scal_ref, g_ref, lsum_ref, pay_ref, own_ref):
    my_x, my_core = scal_ref[0], scal_ref[1]
    parts, held, _ = g_ref.shape
    half_parts = parts // 2
    held -= MEAN_ROWS
    rows = held * half_parts
    for t in range(half_parts):
        for half in range(2):
            block = g_ref[t + half_parts * half].astype(F32)
            mean = block[held : held + 1] + block[held + 1 : held + 2] + block[held + 2 : held + 3]
            own_ref[held * t : held * (t + 1), half * LANES : (half + 1) * LANES] = block[:held] + mean
    full = own_ref[...]
    mean = jnp.sum(full, axis=0, keepdims=True) * (1.0 / rows)
    centred = full - mean
    own_ref[...] = centred
    gram = lax.dot_general(centred, centred, (((0,), (0,)), ((), ())), precision=HIGHEST, preferred_element_type=F32)
    row = lax.broadcasted_iota(I32, (MEANS, LANES), 0) - (4 * my_x + 2 * my_core)
    means = jnp.where(row == 0, mean[:, :LANES], jnp.where(row == 1, mean[:, LANES:], 0.0))
    sums = lsum_ref.shape[0] // 2
    for half in range(2):
        at = my_core ^ half
        pay_ref[at, :LANES] = gram[LANES * half : LANES * (half + 1), LANES * half : LANES * (half + 1)]
        pay_ref[at, LANES:TRIANGLE] = gram[64 * half : 64 * (half + 1), LANES:]
        pay_ref[at, TRIANGLE : TRIANGLE + MEANS] = means
        pay_ref[at, TRIANGLE + MEANS :] = lsum_ref[sums * half : sums * (half + 1)]


def gram_call(scalars, gathered, log_sums, rows):
    return pl.pallas_call(
        gram_kernel,
        in_specs=[pl.BlockSpec(memory_space=pltpu.SMEM)] + [pl.BlockSpec(memory_space=pltpu.VMEM)] * 2,
        out_specs=[pl.BlockSpec(memory_space=pltpu.VMEM)] * 2,
        out_shape=[
            jax.ShapeDtypeStruct((2, TRIANGLE + MEANS + log_sums.shape[0] // 2, LANES), F32),
            jax.ShapeDtypeStruct((rows, SKETCH), F32),
        ],
        compiler_params=pltpu.CompilerParams(vmem_limit_bytes=VMEM_LIMIT),
        name="gram",
    )(scalars, gathered, log_sums)


def stacked(value):
    high, middle, low = three_parts(value)
    left = jnp.concatenate([high, high, middle, high, low, middle], axis=0)
    right = jnp.concatenate([high, middle, high, low, high, middle], axis=0)
    return left, right


def over_rows(left, right):
    return lax.dot_general(left, right, (((0,), (0,)), ((), ())), preferred_element_type=F32)


def eliminate(panel, start):
    count, tile = panel.shape[0], 8
    tiles = count // tile
    lane = lax.broadcasted_iota(I32, (tile, LANES), 1)
    sub = lax.broadcasted_iota(I32, (tile, LANES), 0)
    rows = [panel[tile * t : tile * (t + 1)] for t in range(tiles)]
    spread = [
        [
            jnp.broadcast_to(rows[t][:, start + k : start + k + 1], (tile, LANES)) if t >= k // tile else None
            for t in range(tiles)
        ]
        for k in range(count)
    ]
    halves = []
    for half in range(SKETCH // LANES):
        pieces = [row[:, half * LANES : (half + 1) * LANES] for row in rows]
        if start // LANES == half:
            local = lane - (start - half * LANES)
            for t in range(tiles):
                unit = jnp.where(local == sub + tile * t, 1.0, 0.0)
                pieces[t] = jnp.where((local >= 0) & (local < count), unit, pieces[t])
        halves.append(pieces)
    pivots = [jnp.zeros((tile, LANES), F32) for _ in range(tiles)]
    for j in range(count):
        at, row = j // tile, j % tile
        pivot = jnp.broadcast_to(spread[j][at][row : row + 1], (tile, LANES))
        pivots[at] = jnp.where(sub == row, pivot, pivots[at])
        if j + 1 == count:
            break
        inverse = 1.0 / pivot
        scale = [None if t < at else spread[j][t] * inverse for t in range(tiles)]
        scale[at] = jnp.where(sub > row, scale[at], 0.0)
        for k in range(j + 1, count):
            factor = spread[j][k // tile][k % tile : k % tile + 1]
            for t in range(k // tile, tiles):
                spread[k][t] = spread[k][t] - scale[t] * factor
        for pieces in halves:
            factor = pieces[at][row : row + 1]
            for t in range(at, tiles):
                pieces[t] = pieces[t] - scale[t] * factor
    roots = [lax.rsqrt(pivot) for pivot in pivots]
    return jnp.concatenate(
        [jnp.concatenate([pieces[t] * roots[t] for t in range(tiles)], axis=0) for pieces in halves], axis=1
    )


def basis_kernel(scal_ref, mine_ref, theirs_ref, own_ref, w_hbm, q_ref, bt_ref, w_ref, work, sem):
    fetch = pltpu.make_async_copy(w_hbm, w_ref, sem)
    fetch.start()
    my_x, my_core = scal_ref[0], scal_ref[1]
    size = SKETCH

    @pl.when(my_core >= 0)
    def _():
        mine, theirs = mine_ref[...], theirs_ref[...]
        first = jnp.where(my_core == 0, mine, theirs)
        second = jnp.where(my_core == 0, theirs, mine)
        means = mine[TRIANGLE : TRIANGLE + MEANS]
        mean_rows = [means[2 * d : 2 * d + 2] for d in range(8)]
        centre = sum(mean_rows) * 0.125
        apart = [jnp.concatenate([m[0:1] - centre[0:1], m[1:2] - centre[1:2]], axis=1) for m in mean_rows]
        apart = jnp.concatenate(apart, axis=0)
        docs = own_ref.shape[0]
        shift = over_rows(*stacked(jnp.concatenate([apart, jnp.zeros_like(apart)], axis=0))) * jnp.float32(docs)
        work[:LANES, :LANES] = first[:LANES] + shift[:LANES, :LANES]
        work[:64, LANES:] = first[LANES:TRIANGLE] + shift[:64, LANES:]
        work[64:LANES, LANES:] = second[LANES:TRIANGLE] + shift[64:LANES, LANES:]
        work[LANES:, LANES:] = second[:LANES] + shift[LANES:, LANES:]
        work[LANES:, :LANES] = jnp.zeros((LANES, LANES), F32)
        mean_at = lax.broadcasted_iota(I32, (8, SKETCH), 0) == 2 * my_x + my_core
        own_shift = jnp.sum(jnp.where(mean_at, apart, 0.0), axis=0, keepdims=True)

        for start in range(0, size, PIVOTS):
            rest = start + PIVOTS
            factor_rows = eliminate(work[start:rest, :], start)
            work[start:rest, :] = factor_rows
            if rest < size:
                left, right = stacked(factor_rows)
                from_col = rest // LANES * LANES
                update = over_rows(left[:, from_col:], right)
                old = work[rest:, :]
                column = lax.broadcasted_iota(I32, old.shape, 1)
                old = jnp.where((column >= start) & (column < rest), 0.0, old)
                work[rest:, :] = old - update[rest - from_col :, :]

        row = lax.broadcasted_iota(I32, (size, size), 0)
        column = lax.broadcasted_iota(I32, (size, size), 1)
        inverse = jnp.where(column <= row, work[...], 0.0)
        own = own_ref[...] + own_shift
        contract = (((1,), (1,)), ((), ()))
        q_ref[...] = lax.dot_general(own, inverse, contract, precision=HIGHEST, preferred_element_type=F32)
        flipped = lax.dot_general(inverse, own, contract, precision=HIGHEST, preferred_element_type=F32).astype(BF16)
        rows = size // 8
        for x in range(4):
            place = (x - my_x) & 3
            place = jnp.where(place == 2, 0, jnp.where(place == 3, 2, jnp.where(place == 1, 1, 3)))
            for core in range(2):
                piece = flipped[rows * (2 * x + core) : rows * (2 * x + core + 1)]
                bt_ref[place, (my_core + core) & 1] = piece

    fetch.wait()


def basis_call(scalars, mine, theirs, own, weighted):
    rows = own.shape[0]
    in_vmem = pl.BlockSpec(memory_space=pltpu.VMEM)
    in_hbm = pl.BlockSpec(memory_space=pltpu.HBM)
    return pl.pallas_call(
        basis_kernel,
        in_specs=[pl.BlockSpec(memory_space=pltpu.SMEM)] + [in_vmem] * 3 + [in_hbm],
        out_specs=[in_vmem] * 3,
        out_shape=[
            jax.ShapeDtypeStruct((rows, SKETCH), F32),
            jax.ShapeDtypeStruct((4, 2, SKETCH // 8, rows), BF16),
            pltpu.VMEM(weighted.shape, BF16),
        ],
        scratch_shapes=[pltpu.VMEM((SKETCH, SKETCH), F32), pltpu.SemaphoreType.DMA],
        compiler_params=pltpu.CompilerParams(vmem_limit_bytes=VMEM_LIMIT),
        name="basis",
    )(scalars, mine, theirs, own, pltpu.with_memory_space_constraint(weighted, pltpu.HBM))


def project_kernel(scal_ref, bt_ref, w_ref, centre_ref, idf_ref, mine_ref, theirs_ref, *out_refs, first):
    _, cores, rows, depth = bt_ref.shape
    ours_refs, sibling_refs, mean_ref = out_refs[:-1:2], out_refs[1:-1:2], out_refs[-1]
    pieces = len(ours_refs)
    width = ours_refs[0].shape[1]
    left = bt_ref[first : first + pieces].reshape(pieces * cores * rows, depth)
    sums = jnp.sum(left.astype(F32), axis=1, keepdims=True)
    tail = TRIANGLE + MEANS
    on_first = scal_ref[1] == 0
    low = jnp.where(on_first, mine_ref[tail:], theirs_ref[tail:])
    high = jnp.where(on_first, theirs_ref[tail:], mine_ref[tail:])
    log_mean = jnp.concatenate([low, high], axis=0) * (1.0 / (8 * depth))
    idf = idf_ref[...]
    mean_ref[...] = idf * (1.0 + log_mean)
    apart = idf * (centre_ref[...] - log_mean)
    block = 512
    for at in range(0, width, block):
        product = jnp.dot(left, w_ref[:depth, at : at + block], preferred_element_type=F32)
        row = at // LANES
        shift = jnp.concatenate([apart[row + k : row + k + 1] for k in range(block // LANES)], axis=1)
        product = (product + sums * shift).astype(BF16)
        for k in range(pieces):
            base = k * cores * rows
            ours_refs[k][:, at : at + block] = product[base : base + rows]
            sibling_refs[k][:, at : at + block] = product[base + rows : base + 2 * rows]


def project_call(places, basis, weighted, centres, idf, mine, theirs, first, pieces):
    _, _, rows, _ = basis.shape
    cols = weighted.shape[1]
    in_vmem = pl.BlockSpec(memory_space=pltpu.VMEM)
    return pl.pallas_call(
        functools.partial(project_kernel, first=first),
        in_specs=[pl.BlockSpec(memory_space=pltpu.SMEM)] + [in_vmem] * 6,
        out_specs=[in_vmem] * (2 * pieces + 1),
        out_shape=[jax.ShapeDtypeStruct((rows, cols), BF16)] * (2 * pieces)
        + [jax.ShapeDtypeStruct(centres.shape, F32)],
        compiler_params=pltpu.CompilerParams(vmem_limit_bytes=24 * 1024 * 1024),
        name="project",
    )(places, basis, weighted, centres, idf, mine, theirs)


def swap(value):
    return lax.ppermute(value, "core", [(0, 1), (1, 0)])


def shift_x(value, by):
    return lax.ppermute(value, "x", [(i, (i + by) % 4) for i in range(4)])


def half_sum(a, b):
    return (a.astype(F32) + b.astype(F32)).astype(BF16)


def body(counts, doc_freq, sketch_seed):
    rows, cols = counts.shape
    terms_axes = ("y", "z")
    parts = lax.axis_size(terms_axes)
    my_x, my_core = lax.axis_index("x"), lax.axis_index("core")
    places = jnp.stack([my_x, my_core]).astype(I32)

    sketch_part, weighted, log_sums, centres, idf = sketch_call(sketch_seed, counts, doc_freq, parts)

    pieces = lax.all_to_all(sketch_part, terms_axes, 0, 0)
    gathered = lax.all_to_all(share_call(pieces), terms_axes, 0, 0)
    payload, own = gram_call(places, gathered, log_sums, rows)

    mine = payload[0] + swap(payload[1])
    mine = (mine + shift_x(mine, 2)) + (shift_x(mine, 1) + shift_x(mine, 3))
    theirs = swap(mine)
    basis, flipped, weighted = basis_call(places, mine, theirs, own, weighted)

    operands = (places, flipped, weighted, centres, idf, mine, theirs)
    ours2, other2, means = project_call(*operands, 0, 1)
    opposite = half_sum(ours2, swap(other2))
    flipped, opposite = lax.optimization_barrier((flipped, opposite))
    operands = (places, flipped) + operands[2:]
    ours1, other1, ours3, other3, _ = project_call(*operands, 1, 2)
    flipped, other1, other3 = lax.optimization_barrier((flipped, other1, other3))
    operands = (places, flipped) + operands[2:]
    ours0, other0, _ = project_call(*operands, 3, 1)
    half = cols // 2
    relay_up = shift_x(opposite[:, :half], 1)
    relay_down = shift_x(opposite[:, half:], -1)
    up = ours1.astype(F32) + swap(other1).astype(F32)
    up = jnp.concatenate([up[:, :half] + relay_up.astype(F32), up[:, half:]], axis=1).astype(BF16)
    down = ours3.astype(F32) + swap(other3).astype(F32)
    down = jnp.concatenate([down[:, :half], down[:, half:] + relay_down.astype(F32)], axis=1).astype(BF16)
    total = ours0.astype(F32) + swap(other0).astype(F32)
    total = total + shift_x(up, 1).astype(F32) + shift_x(down, -1).astype(F32)
    return (basis, total.astype(BF16), means.reshape(cols))


def solution(mesh):
    split = Mesh(np.array(mesh.devices).reshape(4, 2, 4, 8), ("x", "core", "y", "z"))
    docs, terms = ("x", "core"), ("y", "z")
    return jax.shard_map(
        body,
        mesh=split,
        in_specs=(P(docs, terms), P(terms), P()),
        out_specs=(P(docs, None), P(docs, terms), P(terms)),
        check_vma=False,
    )
```

```python
import functools
import math

import jax
import jax.numpy as jnp
import numpy as np
from jax import lax
from jax.experimental import pallas as pl
from jax.experimental.pallas import tpu as pltpu
from jax.sharding import Mesh
from jax.sharding import PartitionSpec as P

TERMS = 262144
SKETCH = 256
CORPUS = 2000000000
BYTE_SUM_STD = 147.8
FACTOR = 1.0 / (BYTE_SUM_STD * TERMS**0.5)
HIGHEST = lax.Precision.HIGHEST
F32, BF16, I32 = jnp.float32, jnp.bfloat16, jnp.int32
VMEM_LIMIT = 16 * 1024 * 1024
LANES = 128
PIVOTS = 32
TAIL = 16
MEAN_ROWS = 8
TRIANGLE = 192
MEANS = 16


def log_count(counts):
    return jnp.log(jnp.maximum(counts.astype(F32), math.exp(-1.0)))


def idf_of(doc_freq):
    return 1.0 + jnp.log(jnp.float32(CORPUS) / doc_freq.astype(F32))


def three_parts(value):
    high = value.astype(BF16)
    rest = value - high.astype(F32)
    middle = rest.astype(BF16)
    low = (rest - middle.astype(F32)).astype(BF16)
    return high, middle, low


def parts_tile(value, rows):
    high, middle, low = (part.astype(F32) for part in three_parts(value))
    where = lax.broadcasted_iota(I32, (rows, value.shape[1]), 0)
    tile = jnp.where(where == 0, high, jnp.where(where == 1, middle, jnp.where(where == 2, low, 0.0)))
    return tile.astype(BF16)


def sketch_kernel(
    seed_ref, counts_hbm, df_hbm, s_ref, w_hbm, lsum_ref, centre_ref, idf, counts, df, om, wb, in_sems, out_sems, df_sem
):
    rows, cols = counts_hbm.shape
    strip = rows // in_sems.shape[0]
    chunk = cols // out_sems.shape[0]

    def load(i):
        at = pl.ds(i * strip, strip)
        return pltpu.make_async_copy(counts_hbm.at[at], counts.at[at], in_sems.at[i])

    def store(i):
        at = pl.ds(pl.multiple_of(i * chunk, chunk), chunk)
        return pltpu.make_async_copy(wb.at[:, at], w_hbm.at[:, at], out_sems.at[i])

    load_df = pltpu.make_async_copy(df_hbm, df, df_sem)
    load_df.start()
    for i in range(rows // strip):
        load(i).start()

    first = lax.axis_index(("y", "z")) * (cols * SKETCH)
    key = seed_ref[0] * 668265263
    low_key, high_key = key & 255, key & -256
    lane = lax.broadcasted_iota(I32, (1, LANES), 1)
    col_parts = [((lane + half * LANES) ^ low_key) * 1640531527 for half in range(SKETCH // LANES)]
    group = 256
    local = lax.broadcasted_iota(I32, (group, LANES), 0) * SKETCH + first

    def hash_rows(g, carry):
        row_part = ((local + g * (group * SKETCH)) ^ high_key) * 1640531527
        for half, col_part in enumerate(col_parts):
            h = row_part + col_part
            h = h ^ lax.shift_right_logical(h, jnp.int32(15))
            h = h * 739982445
            h = h ^ lax.shift_right_logical(h, jnp.int32(13))
            pair = (h & 0x00FF00FF) + (lax.shift_right_logical(h, jnp.int32(8)) & 0x00FF00FF)
            byte_sum = lax.shift_right_logical(pair * 65537, jnp.int32(16))
            value = (byte_sum - 510).astype(F32).astype(BF16)
            om[pl.ds(pl.multiple_of(g * group, group), group), half * LANES : (half + 1) * LANES] = value
        return carry

    lax.fori_loop(0, cols // group, hash_rows, 0)

    load_df.wait()
    idf[...] = idf_of(df[...])
    for i in range(rows // strip):
        load(i).wait()

    strip_rows = 32

    def weigh(tile):
        at = pl.ds(pl.multiple_of(tile * LANES, LANES), LANES)
        part = log_count(counts[:strip_rows, at])
        centre = jnp.sum(part, axis=0, keepdims=True) * (1.0 / strip_rows)
        scale = idf[pl.ds(tile, 1), :]
        wb[:strip_rows, at] = ((part - centre) * scale).astype(BF16)
        wb[rows:, at] = parts_tile(scale * (1.0 + centre), TAIL)
        centre_ref[pl.ds(tile, 1), :] = centre
        for r in range(strip_rows, rows, strip_rows):
            values = log_count(counts[r : r + strip_rows, at])
            part = part + values
            wb[r : r + strip_rows, at] = ((values - centre) * scale).astype(BF16)
        lsum_ref[pl.ds(tile, 1), :] = jnp.sum(part, axis=0, keepdims=True)

    def weigh_chunk(i, carry):
        per_chunk = chunk // LANES

        def one(k, c):
            weigh(i * per_chunk + k)
            return c

        lax.fori_loop(0, per_chunk, one, 0, unroll=2)
        store(i).start()
        return carry

    lax.fori_loop(0, cols // chunk, weigh_chunk, 0)

    product = jnp.dot(wb[...], om[...], preferred_element_type=F32) * FACTOR
    centre = jnp.sum(product[rows:, :], axis=0, keepdims=True)
    shares = s_ref.shape[0] // 2
    share = rows // shares
    for half in range(SKETCH // LANES):
        at = slice(half * LANES, (half + 1) * LANES)
        tail = parts_tile(centre[:, at], MEAN_ROWS).astype(F32)
        for t in range(shares):
            value = jnp.concatenate([product[share * t : share * (t + 1), at], tail], axis=0)
            s_ref[shares * half + t] = value.astype(BF16)
    for i in range(cols // chunk):
        store(i).wait()


def sketch_call(seed, counts, doc_freq, parts):
    rows, cols = counts.shape
    in_vmem = pl.BlockSpec(memory_space=pltpu.VMEM)
    in_hbm = pl.BlockSpec(memory_space=pltpu.HBM)
    return pl.pallas_call(
        sketch_kernel,
        in_specs=[pl.BlockSpec(memory_space=pltpu.SMEM), in_hbm, in_hbm],
        out_specs=[in_vmem, in_hbm, in_vmem, in_vmem, in_vmem],
        out_shape=[
            pltpu.VMEM((parts, 2 * rows // parts + MEAN_ROWS, LANES), BF16),
            pltpu.HBM((rows + TAIL, cols), BF16),
        ]
        + [jax.ShapeDtypeStruct((cols // LANES, LANES), F32)] * 3,
        scratch_shapes=[
            pltpu.VMEM((rows, cols), I32),
            pltpu.VMEM((cols // LANES, LANES), I32),
            pltpu.VMEM((cols, SKETCH), BF16),
            pltpu.VMEM((rows + TAIL, cols), BF16),
            pltpu.SemaphoreType.DMA((8,)),
            pltpu.SemaphoreType.DMA((8,)),
            pltpu.SemaphoreType.DMA,
        ],
        compiler_params=pltpu.CompilerParams(vmem_limit_bytes=40 * 1024 * 1024),
        name="sketch",
    )(
        seed,
        pltpu.with_memory_space_constraint(counts, pltpu.HBM),
        pltpu.with_memory_space_constraint(doc_freq.reshape(cols // LANES, LANES), pltpu.HBM),
    )


def share_kernel(pieces_ref, out_ref):
    total = pieces_ref[0].astype(F32)
    for t in range(1, pieces_ref.shape[0]):
        total = total + pieces_ref[t].astype(F32)
    held = total.shape[0] - MEAN_ROWS
    centre = total[held : held + 1] + total[held + 1 : held + 2] + total[held + 2 : held + 3]
    value = jnp.concatenate([total[:held], parts_tile(centre, MEAN_ROWS).astype(F32)], axis=0).astype(BF16)
    for t in range(out_ref.shape[0]):
        out_ref[t] = value


def share_call(pieces):
    return pl.pallas_call(
        share_kernel,
        in_specs=[pl.BlockSpec(memory_space=pltpu.VMEM)],
        out_specs=pl.BlockSpec(memory_space=pltpu.VMEM),
        out_shape=pltpu.VMEM(pieces.shape, BF16),
        compiler_params=pltpu.CompilerParams(vmem_limit_bytes=VMEM_LIMIT),
        name="share",
    )(pieces)


def gram_kernel(g_ref, lsum_ref, pay_ref, own_ref):
    my_x, my_core = lax.axis_index("x"), lax.axis_index("core")
    parts, held, _ = g_ref.shape
    half_parts = parts // 2
    held -= MEAN_ROWS
    rows = held * half_parts
    for t in range(half_parts):
        for half in range(2):
            block = g_ref[t + half_parts * half].astype(F32)
            mean = block[held : held + 1] + block[held + 1 : held + 2] + block[held + 2 : held + 3]
            own_ref[held * t : held * (t + 1), half * LANES : (half + 1) * LANES] = block[:held] + mean
    full = own_ref[...]
    mean = jnp.sum(full, axis=0, keepdims=True) * (1.0 / rows)
    centred = full - mean
    own_ref[...] = centred
    gram = lax.dot_general(centred, centred, (((0,), (0,)), ((), ())), precision=HIGHEST, preferred_element_type=F32)
    row = lax.broadcasted_iota(I32, (MEANS, LANES), 0) - (4 * my_x + 2 * my_core)
    means = jnp.where(row == 0, mean[:, :LANES], jnp.where(row == 1, mean[:, LANES:], 0.0))
    sums = lsum_ref.shape[0] // 2
    for half in range(2):
        at = my_core ^ half
        pay_ref[at, :LANES] = gram[LANES * half : LANES * (half + 1), LANES * half : LANES * (half + 1)]
        pay_ref[at, LANES:TRIANGLE] = gram[64 * half : 64 * (half + 1), LANES:]
        pay_ref[at, TRIANGLE : TRIANGLE + MEANS] = means
        pay_ref[at, TRIANGLE + MEANS :] = lsum_ref[sums * half : sums * (half + 1)]


def gram_call(gathered, log_sums, rows):
    return pl.pallas_call(
        gram_kernel,
        in_specs=[pl.BlockSpec(memory_space=pltpu.VMEM)] * 2,
        out_specs=[pl.BlockSpec(memory_space=pltpu.VMEM)] * 2,
        out_shape=[
            jax.ShapeDtypeStruct((2, TRIANGLE + MEANS + log_sums.shape[0] // 2, LANES), F32),
            jax.ShapeDtypeStruct((rows, SKETCH), F32),
        ],
        compiler_params=pltpu.CompilerParams(vmem_limit_bytes=VMEM_LIMIT),
        name="gram",
    )(gathered, log_sums)


def stacked(value):
    high, middle, low = three_parts(value)
    left = jnp.concatenate([high, high, middle, high, low, middle], axis=0)
    right = jnp.concatenate([high, middle, high, low, high, middle], axis=0)
    return left, right


def over_rows(left, right):
    return lax.dot_general(left, right, (((0,), (0,)), ((), ())), preferred_element_type=F32)


def by_rows(left, right):
    return lax.dot_general(left, right, (((1,), (1,)), ((), ())), precision=HIGHEST, preferred_element_type=F32)


def eliminate(panel, start):
    count, tile = panel.shape[0], 8
    tiles = count // tile
    lane = lax.broadcasted_iota(I32, (tile, LANES), 1)
    sub = lax.broadcasted_iota(I32, (tile, LANES), 0)
    rows = [panel[tile * t : tile * (t + 1)] for t in range(tiles)]
    spread = [
        [
            jnp.broadcast_to(rows[t][:, start + k : start + k + 1], (tile, LANES)) if t >= k // tile else None
            for t in range(tiles)
        ]
        for k in range(count)
    ]
    halves = []
    for half in range(SKETCH // LANES):
        pieces = [row[:, half * LANES : (half + 1) * LANES] for row in rows]
        if start // LANES == half:
            local = lane - (start - half * LANES)
            for t in range(tiles):
                unit = jnp.where(local == sub + tile * t, 1.0, 0.0)
                pieces[t] = jnp.where((local >= 0) & (local < count), unit, pieces[t])
        halves.append(pieces)
    pivots = [jnp.zeros((tile, LANES), F32) for _ in range(tiles)]
    for j in range(count):
        at, row = j // tile, j % tile
        pivot = jnp.broadcast_to(spread[j][at][row : row + 1], (tile, LANES))
        pivots[at] = jnp.where(sub == row, pivot, pivots[at])
        if j + 1 == count:
            break
        inverse = 1.0 / pivot
        scale = [None if t < at else spread[j][t] * inverse for t in range(tiles)]
        scale[at] = jnp.where(sub > row, scale[at], 0.0)
        for k in range(j + 1, count):
            factor = spread[j][k // tile][k % tile : k % tile + 1]
            for t in range(k // tile, tiles):
                spread[k][t] = spread[k][t] - scale[t] * factor
        for pieces in halves:
            factor = pieces[at][row : row + 1]
            for t in range(at, tiles):
                pieces[t] = pieces[t] - scale[t] * factor
    roots = [lax.rsqrt(pivot) for pivot in pivots]
    return jnp.concatenate(
        [jnp.concatenate([pieces[t] * roots[t] for t in range(tiles)], axis=0) for pieces in halves], axis=1
    )


def basis_kernel(mine_ref, theirs_ref, own_ref, w_hbm, inverse_ref, shifted_ref, bt_ref, w_ref, work, sem):
    fetch = pltpu.make_async_copy(w_hbm, w_ref, sem)
    fetch.start()
    my_x, my_core = lax.axis_index("x"), lax.axis_index("core")
    size = SKETCH

    @pl.when(my_core >= 0)
    def _():
        mine, theirs = mine_ref[...], theirs_ref[...]
        first = jnp.where(my_core == 0, mine, theirs)
        second = jnp.where(my_core == 0, theirs, mine)
        means = mine[TRIANGLE : TRIANGLE + MEANS]
        mean_rows = [means[2 * d : 2 * d + 2] for d in range(8)]
        centre = sum(mean_rows) * 0.125
        apart = [jnp.concatenate([m[0:1] - centre[0:1], m[1:2] - centre[1:2]], axis=1) for m in mean_rows]
        apart = jnp.concatenate(apart, axis=0)
        docs = own_ref.shape[0]
        shift = over_rows(*stacked(jnp.concatenate([apart, jnp.zeros_like(apart)], axis=0))) * jnp.float32(docs)
        work[:LANES, :LANES] = first[:LANES] + shift[:LANES, :LANES]
        work[:64, LANES:] = first[LANES:TRIANGLE] + shift[:64, LANES:]
        work[64:LANES, LANES:] = second[LANES:TRIANGLE] + shift[64:LANES, LANES:]
        work[LANES:, LANES:] = second[:LANES] + shift[LANES:, LANES:]
        work[LANES:, :LANES] = jnp.zeros((LANES, LANES), F32)
        mean_at = lax.broadcasted_iota(I32, (8, SKETCH), 0) == 2 * my_x + my_core
        own_shift = jnp.sum(jnp.where(mean_at, apart, 0.0), axis=0, keepdims=True)

        for start in range(0, size, PIVOTS):
            rest = start + PIVOTS
            factor_rows = eliminate(work[start:rest, :], start)
            work[start:rest, :] = factor_rows
            if rest < size:
                left, right = stacked(factor_rows)
                from_col = rest // LANES * LANES
                update = over_rows(left[:, from_col:], right)
                old = work[rest:, :]
                column = lax.broadcasted_iota(I32, old.shape, 1)
                old = jnp.where((column >= start) & (column < rest), 0.0, old)
                work[rest:, :] = old - update[rest - from_col :, :]

        row = lax.broadcasted_iota(I32, (size, size), 0)
        column = lax.broadcasted_iota(I32, (size, size), 1)
        inverse = jnp.where(column <= row, work[...], 0.0)
        own = own_ref[...] + own_shift
        inverse_ref[...] = inverse
        shifted_ref[...] = own
        flipped = by_rows(inverse, own).astype(BF16)
        rows = size // 8
        for x in range(4):
            place = (x - my_x) & 3
            place = jnp.where(place == 2, 0, jnp.where(place == 3, 2, jnp.where(place == 1, 1, 3)))
            for core in range(2):
                piece = flipped[rows * (2 * x + core) : rows * (2 * x + core + 1)]
                bt_ref[place, (my_core + core) & 1] = piece

    fetch.wait()


def basis_call(mine, theirs, own, weighted):
    rows = own.shape[0]
    in_vmem = pl.BlockSpec(memory_space=pltpu.VMEM)
    in_hbm = pl.BlockSpec(memory_space=pltpu.HBM)
    return pl.pallas_call(
        basis_kernel,
        in_specs=[in_vmem] * 3 + [in_hbm],
        out_specs=[in_vmem] * 4,
        out_shape=[
            jax.ShapeDtypeStruct((SKETCH, SKETCH), F32),
            jax.ShapeDtypeStruct((rows, SKETCH), F32),
            jax.ShapeDtypeStruct((4, 2, SKETCH // 8, rows), BF16),
            pltpu.VMEM(weighted.shape, BF16),
        ],
        scratch_shapes=[pltpu.VMEM((SKETCH, SKETCH), F32), pltpu.SemaphoreType.DMA],
        compiler_params=pltpu.CompilerParams(vmem_limit_bytes=VMEM_LIMIT),
        name="basis",
    )(mine, theirs, own, pltpu.with_memory_space_constraint(weighted, pltpu.HBM))


def log_means(mine_ref, theirs_ref, docs):
    tail = TRIANGLE + MEANS
    on_first = lax.axis_index("core") == 0
    low = jnp.where(on_first, mine_ref[tail:], theirs_ref[tail:])
    high = jnp.where(on_first, theirs_ref[tail:], mine_ref[tail:])
    return jnp.concatenate([low, high], axis=0) * (1.0 / docs)


def project_kernel(bt_ref, w_ref, centre_ref, idf_ref, mine_ref, theirs_ref, *out_refs, first, pieces, cut):
    _, cores, rows, depth = bt_ref.shape
    width = w_ref.shape[1]
    left = bt_ref[first : first + pieces].reshape(pieces * cores * rows, depth)
    sums = jnp.sum(left.astype(F32), axis=1, keepdims=True)
    apart = idf_ref[...] * (centre_ref[...] - log_means(mine_ref, theirs_ref, 8 * depth))
    block = 512
    for at in range(0, width, block):
        product = jnp.dot(left, w_ref[:depth, at : at + block], preferred_element_type=F32)
        row = at // LANES
        shift = jnp.concatenate([apart[row + k : row + k + 1] for k in range(block // LANES)], axis=1)
        product = (product + sums * shift).astype(BF16)
        for k in range(pieces * cores):
            value = product[k * rows : (k + 1) * rows]
            if not cut:
                out_refs[k][:, at : at + block] = value
            elif k >= cores:
                out_refs[cores + k][:, at : at + block] = value
            else:
                begin = at % (width // 2)
                out_refs[2 * (2 * at // width) + k][:, begin : begin + block] = value


def project_last_kernel(own_ref, inverse_ref, bt_ref, w_ref, centre_ref, idf_ref, mine_ref, theirs_ref, *out_refs):
    q_ref, mean_ref = out_refs[2:]
    q_ref[...] = by_rows(own_ref[...], inverse_ref[...])
    docs = 8 * own_ref.shape[0]
    mean_ref[...] = idf_ref[...] * (1.0 + log_means(mine_ref, theirs_ref, docs))
    project_kernel(
        bt_ref, w_ref, centre_ref, idf_ref, mine_ref, theirs_ref, *out_refs[:2], first=3, pieces=1, cut=False
    )


def project_call(kernel, outs, operands):
    in_vmem = pl.BlockSpec(memory_space=pltpu.VMEM)
    return pl.pallas_call(
        kernel,
        in_specs=[in_vmem] * len(operands),
        out_specs=[in_vmem] * len(outs),
        out_shape=outs,
        compiler_params=pltpu.CompilerParams(vmem_limit_bytes=24 * 1024 * 1024),
        name="project",
    )(*operands)


def swap(value):
    return lax.ppermute(value, "core", [(0, 1), (1, 0)])


def shift_x(value, by):
    return lax.ppermute(value, "x", [(i, (i + by) % 4) for i in range(4)])


def half_sum(a, b):
    return (a.astype(F32) + b.astype(F32)).astype(BF16)


def body(counts, doc_freq, sketch_seed):
    rows, cols = counts.shape
    terms_axes = ("y", "z")
    parts = lax.axis_size(terms_axes)

    sketch_part, weighted, log_sums, centres, idf = sketch_call(sketch_seed, counts, doc_freq, parts)

    pieces = lax.all_to_all(sketch_part, terms_axes, 0, 0)
    gathered = lax.all_to_all(share_call(pieces), terms_axes, 0, 0)
    payload, own = gram_call(gathered, log_sums, rows)

    mine = payload[0] + swap(payload[1])
    mine = (mine + shift_x(mine, 2)) + (shift_x(mine, 1) + shift_x(mine, 3))
    theirs = swap(mine)
    inverse, own, flipped, weighted = basis_call(mine, theirs, own, weighted)

    half = cols // 2
    narrow, wide = (jax.ShapeDtypeStruct((SKETCH // 8, n), BF16) for n in (half, cols))
    rest = (weighted, centres, idf, mine, theirs)
    ours2a, other2a, ours2b, other2b, ours1, other1, ours3, other3 = project_call(
        functools.partial(project_kernel, first=0, pieces=3, cut=True), [narrow] * 4 + [wide] * 4, (flipped,) + rest
    )
    relay_up = shift_x(half_sum(ours2a, swap(other2a)), 1)
    relay_down = shift_x(half_sum(ours2b, swap(other2b)), -1)
    theirs1, theirs3 = swap(other1), swap(other3)
    up = ours1.astype(F32) + theirs1.astype(F32)
    up = jnp.concatenate([up[:, :half] + relay_up.astype(F32), up[:, half:]], axis=1).astype(BF16)
    down = ours3.astype(F32) + theirs3.astype(F32)
    down = jnp.concatenate([down[:, :half], down[:, half:] + relay_down.astype(F32)], axis=1).astype(BF16)
    from_below, from_above = shift_x(up, 1), shift_x(down, -1)
    flipped, _, _ = lax.optimization_barrier((flipped, theirs1, theirs3))
    ours0, other0, basis, means = project_call(
        project_last_kernel,
        [wide, wide, jax.ShapeDtypeStruct(own.shape, F32), jax.ShapeDtypeStruct(idf.shape, F32)],
        (own, inverse, flipped) + rest,
    )
    total = ours0.astype(F32) + swap(other0).astype(F32)
    total = total + from_below.astype(F32) + from_above.astype(F32)
    return (basis, total.astype(BF16), means.reshape(cols))


def solution(mesh):
    split = Mesh(np.array(mesh.devices).reshape(4, 2, 4, 8), ("x", "core", "y", "z"))
    docs, terms = ("x", "core"), ("y", "z")
    return jax.shard_map(
        body,
        mesh=split,
        in_specs=(P(docs, terms), P(terms), P()),
        out_specs=(P(docs, None), P(docs, terms), P(terms)),
        check_vma=False,
    )
```

```python
import functools
import math

import jax
import jax.numpy as jnp
import numpy as np
from jax import lax
from jax.experimental import pallas as pl
from jax.experimental.pallas import tpu as pltpu
from jax.sharding import Mesh
from jax.sharding import PartitionSpec as P

TERMS = 262144
SKETCH = 256
CORPUS = 2000000000
BYTE_SUM_STD = 147.8
FACTOR = 1.0 / (BYTE_SUM_STD * TERMS**0.5)
HIGHEST = lax.Precision.HIGHEST
F32, BF16, I32 = jnp.float32, jnp.bfloat16, jnp.int32
VMEM_LIMIT = 16 * 1024 * 1024
LANES = 128
PIVOTS = 32
TAIL = 16
MEAN_ROWS = 8
TRIANGLE = 160
MEANS = 16


def log_count(counts):
    return jnp.log(jnp.maximum(counts.astype(F32), math.exp(-1.0)))


def idf_of(doc_freq):
    return 1.0 + jnp.log(jnp.float32(CORPUS) / doc_freq.astype(F32))


def three_parts(value):
    high = value.astype(BF16)
    rest = value - high.astype(F32)
    middle = rest.astype(BF16)
    low = (rest - middle.astype(F32)).astype(BF16)
    return high, middle, low


def parts_tile(value, rows):
    high, middle, low = (part.astype(F32) for part in three_parts(value))
    where = lax.broadcasted_iota(I32, (rows, value.shape[1]), 0)
    tile = jnp.where(where == 0, high, jnp.where(where == 1, middle, jnp.where(where == 2, low, 0.0)))
    return tile.astype(BF16)


def sketch_kernel(
    seed_ref, counts_hbm, df_hbm, s_ref, w_hbm, lsum_ref, centre_ref, idf, counts, df, om, wb, in_sems, out_sems, df_sem
):
    rows, cols = counts_hbm.shape
    strip = rows // in_sems.shape[0]
    chunk = cols // out_sems.shape[0]

    def load(i):
        at = pl.ds(i * strip, strip)
        return pltpu.make_async_copy(counts_hbm.at[at], counts.at[at], in_sems.at[i])

    def store(i):
        at = pl.ds(pl.multiple_of(i * chunk, chunk), chunk)
        return pltpu.make_async_copy(wb.at[:, at], w_hbm.at[:, at], out_sems.at[i])

    load_df = pltpu.make_async_copy(df_hbm, df, df_sem)
    load_df.start()
    for i in range(rows // strip):
        load(i).start()

    first = lax.axis_index(("y", "z")) * (cols * SKETCH)
    key = seed_ref[0] * 668265263
    low_key, high_key = key & 255, key & -256
    lane = lax.broadcasted_iota(I32, (1, LANES), 1)
    col_parts = [((lane + half * LANES) ^ low_key) * 1640531527 for half in range(SKETCH // LANES)]
    group = 256
    local = lax.broadcasted_iota(I32, (group, LANES), 0) * SKETCH + first

    def hash_rows(g, carry):
        row_part = ((local + g * (group * SKETCH)) ^ high_key) * 1640531527
        for half, col_part in enumerate(col_parts):
            h = row_part + col_part
            h = h ^ lax.shift_right_logical(h, jnp.int32(15))
            h = h * 739982445
            h = h ^ lax.shift_right_logical(h, jnp.int32(13))
            pair = (h & 0x00FF00FF) + (lax.shift_right_logical(h, jnp.int32(8)) & 0x00FF00FF)
            byte_sum = lax.shift_right_logical(pair * 65537, jnp.int32(16))
            value = (byte_sum - 510).astype(F32).astype(BF16)
            om[pl.ds(pl.multiple_of(g * group, group), group), half * LANES : (half + 1) * LANES] = value
        return carry

    lax.fori_loop(0, cols // group, hash_rows, 0)

    load_df.wait()
    idf[...] = idf_of(df[...])
    for i in range(rows // strip):
        load(i).wait()

    strip_rows = 32

    def weigh(tile):
        at = pl.ds(pl.multiple_of(tile * LANES, LANES), LANES)
        part = log_count(counts[:strip_rows, at])
        centre = jnp.sum(part, axis=0, keepdims=True) * (1.0 / strip_rows)
        scale = idf[pl.ds(tile, 1), :]
        wb[:strip_rows, at] = ((part - centre) * scale).astype(BF16)
        wb[rows:, at] = parts_tile(scale * (1.0 + centre), TAIL)
        centre_ref[pl.ds(tile, 1), :] = centre
        for r in range(strip_rows, rows, strip_rows):
            values = log_count(counts[r : r + strip_rows, at])
            part = part + values
            wb[r : r + strip_rows, at] = ((values - centre) * scale).astype(BF16)
        lsum_ref[pl.ds(tile, 1), :] = jnp.sum(part, axis=0, keepdims=True)

    def weigh_chunk(i, carry):
        per_chunk = chunk // LANES

        def one(k, c):
            weigh(i * per_chunk + k)
            return c

        lax.fori_loop(0, per_chunk, one, 0, unroll=2)
        store(i).start()
        return carry

    lax.fori_loop(0, cols // chunk, weigh_chunk, 0)

    product = jnp.dot(wb[...], om[...], preferred_element_type=F32) * FACTOR
    centre = jnp.sum(product[rows:, :], axis=0, keepdims=True)
    shares = s_ref.shape[0] // 2
    share = rows // shares
    for half in range(SKETCH // LANES):
        at = slice(half * LANES, (half + 1) * LANES)
        tail = parts_tile(centre[:, at], MEAN_ROWS).astype(F32)
        for t in range(shares):
            value = jnp.concatenate([product[share * t : share * (t + 1), at], tail], axis=0)
            s_ref[shares * half + t] = value.astype(BF16)
    for i in range(cols // chunk):
        store(i).wait()


def sketch_call(seed, counts, doc_freq, parts):
    rows, cols = counts.shape
    in_vmem = pl.BlockSpec(memory_space=pltpu.VMEM)
    in_hbm = pl.BlockSpec(memory_space=pltpu.HBM)
    return pl.pallas_call(
        sketch_kernel,
        in_specs=[pl.BlockSpec(memory_space=pltpu.SMEM), in_hbm, in_hbm],
        out_specs=[in_vmem, in_hbm, in_vmem, in_vmem, in_vmem],
        out_shape=[
            pltpu.VMEM((parts, 2 * rows // parts + MEAN_ROWS, LANES), BF16),
            pltpu.HBM((rows + TAIL, cols), BF16),
        ]
        + [jax.ShapeDtypeStruct((cols // LANES, LANES), F32)] * 3,
        scratch_shapes=[
            pltpu.VMEM((rows, cols), I32),
            pltpu.VMEM((cols // LANES, LANES), I32),
            pltpu.VMEM((cols, SKETCH), BF16),
            pltpu.VMEM((rows + TAIL, cols), BF16),
            pltpu.SemaphoreType.DMA((8,)),
            pltpu.SemaphoreType.DMA((8,)),
            pltpu.SemaphoreType.DMA,
        ],
        compiler_params=pltpu.CompilerParams(vmem_limit_bytes=40 * 1024 * 1024),
        name="sketch",
    )(
        seed,
        pltpu.with_memory_space_constraint(counts, pltpu.HBM),
        pltpu.with_memory_space_constraint(doc_freq.reshape(cols // LANES, LANES), pltpu.HBM),
    )


def share_kernel(pieces_ref, out_ref):
    total = pieces_ref[0].astype(F32)
    for t in range(1, pieces_ref.shape[0]):
        total = total + pieces_ref[t].astype(F32)
    held = total.shape[0] - MEAN_ROWS
    centre = total[held : held + 1] + total[held + 1 : held + 2] + total[held + 2 : held + 3]
    value = jnp.concatenate([total[:held], parts_tile(centre, MEAN_ROWS).astype(F32)], axis=0).astype(BF16)
    for t in range(out_ref.shape[0]):
        out_ref[t] = value


def share_call(pieces):
    return pl.pallas_call(
        share_kernel,
        in_specs=[pl.BlockSpec(memory_space=pltpu.VMEM)],
        out_specs=pl.BlockSpec(memory_space=pltpu.VMEM),
        out_shape=pltpu.VMEM(pieces.shape, BF16),
        compiler_params=pltpu.CompilerParams(vmem_limit_bytes=VMEM_LIMIT),
        name="share",
    )(pieces)


def fold(block):
    right = lax.broadcasted_iota(I32, (32, LANES), 1) >= 64
    return jnp.concatenate([block[:64], jnp.where(right, block[64:96], pltpu.roll(block[96:], 64, 1))], axis=0)


def unfold(rows):
    right = lax.broadcasted_iota(I32, (32, LANES), 1) >= 64
    folded = rows[64:96]
    upper, lower = jnp.where(right, folded, 0.0), jnp.where(right, pltpu.roll(folded, 64, 1), 0.0)
    return jnp.concatenate([rows[:64], upper, lower], axis=0)


def gram_kernel(g_ref, lsum_ref, pay_ref, own_ref):
    my_x, my_core = lax.axis_index("x"), lax.axis_index("core")
    parts, held, _ = g_ref.shape
    half_parts = parts // 2
    held -= MEAN_ROWS
    rows = held * half_parts
    for t in range(half_parts):
        for half in range(2):
            block = g_ref[t + half_parts * half].astype(F32)
            mean = block[held : held + 1] + block[held + 1 : held + 2] + block[held + 2 : held + 3]
            own_ref[held * t : held * (t + 1), half * LANES : (half + 1) * LANES] = block[:held] + mean
    full = own_ref[...]
    mean = jnp.sum(full, axis=0, keepdims=True) * (1.0 / rows)
    centred = full - mean
    own_ref[...] = centred
    gram = lax.dot_general(centred, centred, (((0,), (0,)), ((), ())), precision=HIGHEST, preferred_element_type=F32)
    row = lax.broadcasted_iota(I32, (MEANS, LANES), 0) - (4 * my_x + 2 * my_core)
    means = jnp.where(row == 0, mean[:, :LANES], jnp.where(row == 1, mean[:, LANES:], 0.0))
    sums = lsum_ref.shape[0] // 2
    for half in range(2):
        at = my_core ^ half
        pay_ref[at, :96] = fold(gram[LANES * half : LANES * (half + 1), LANES * half : LANES * (half + 1)])
        pay_ref[at, 96:TRIANGLE] = gram[64 * half : 64 * (half + 1), LANES:]
        pay_ref[at, TRIANGLE : TRIANGLE + MEANS] = means
        pay_ref[at, TRIANGLE + MEANS :] = lsum_ref[sums * half : sums * (half + 1)]


def gram_call(gathered, log_sums, rows):
    return pl.pallas_call(
        gram_kernel,
        in_specs=[pl.BlockSpec(memory_space=pltpu.VMEM)] * 2,
        out_specs=[pl.BlockSpec(memory_space=pltpu.VMEM)] * 2,
        out_shape=[
            jax.ShapeDtypeStruct((2, TRIANGLE + MEANS + log_sums.shape[0] // 2, LANES), F32),
            jax.ShapeDtypeStruct((rows, SKETCH), F32),
        ],
        compiler_params=pltpu.CompilerParams(vmem_limit_bytes=VMEM_LIMIT),
        name="gram",
    )(gathered, log_sums)


def stacked(value):
    high, middle, low = three_parts(value)
    left = jnp.concatenate([high, high, middle, high, low, middle], axis=0)
    right = jnp.concatenate([high, middle, high, low, high, middle], axis=0)
    return left, right


def over_rows(left, right):
    return lax.dot_general(left, right, (((0,), (0,)), ((), ())), preferred_element_type=F32)


def by_rows(left, right):
    return lax.dot_general(left, right, (((1,), (1,)), ((), ())), precision=HIGHEST, preferred_element_type=F32)


def eliminate(panel, start):
    count, tile = panel.shape[0], 8
    tiles = count // tile
    lane = lax.broadcasted_iota(I32, (tile, LANES), 1)
    sub = lax.broadcasted_iota(I32, (tile, LANES), 0)
    rows = [panel[tile * t : tile * (t + 1)] for t in range(tiles)]
    spread = [
        [
            jnp.broadcast_to(rows[t][:, start + k : start + k + 1], (tile, LANES)) if t >= k // tile else None
            for t in range(tiles)
        ]
        for k in range(count)
    ]
    halves = []
    for half in range(SKETCH // LANES):
        pieces = [row[:, half * LANES : (half + 1) * LANES] for row in rows]
        if start // LANES == half:
            local = lane - (start - half * LANES)
            for t in range(tiles):
                unit = jnp.where(local == sub + tile * t, 1.0, 0.0)
                pieces[t] = jnp.where((local >= 0) & (local < count), unit, pieces[t])
        halves.append(pieces)
    pivots = [jnp.zeros((tile, LANES), F32) for _ in range(tiles)]
    for j in range(count):
        at, row = j // tile, j % tile
        pivot = jnp.broadcast_to(spread[j][at][row : row + 1], (tile, LANES))
        pivots[at] = jnp.where(sub == row, pivot, pivots[at])
        if j + 1 == count:
            break
        inverse = 1.0 / pivot
        scale = [None if t < at else spread[j][t] * inverse for t in range(tiles)]
        scale[at] = jnp.where(sub > row, scale[at], 0.0)
        for k in range(j + 1, count):
            factor = spread[j][k // tile][k % tile : k % tile + 1]
            for t in range(k // tile, tiles):
                spread[k][t] = spread[k][t] - scale[t] * factor
        for pieces in halves:
            factor = pieces[at][row : row + 1]
            for t in range(at, tiles):
                pieces[t] = pieces[t] - scale[t] * factor
    roots = [lax.rsqrt(pivot) for pivot in pivots]
    return jnp.concatenate(
        [jnp.concatenate([pieces[t] * roots[t] for t in range(tiles)], axis=0) for pieces in halves], axis=1
    )


def basis_kernel(mine_ref, theirs_ref, own_ref, w_hbm, inverse_ref, shifted_ref, bt_ref, w_ref, work, sem):
    fetch = pltpu.make_async_copy(w_hbm, w_ref, sem)
    fetch.start()
    my_x, my_core = lax.axis_index("x"), lax.axis_index("core")
    size = SKETCH

    @pl.when(my_core >= 0)
    def _():
        mine, theirs = mine_ref[...], theirs_ref[...]
        first = jnp.where(my_core == 0, mine, theirs)
        second = jnp.where(my_core == 0, theirs, mine)
        means = mine[TRIANGLE : TRIANGLE + MEANS]
        mean_rows = [means[2 * d : 2 * d + 2] for d in range(8)]
        centre = sum(mean_rows) * 0.125
        apart = [jnp.concatenate([m[0:1] - centre[0:1], m[1:2] - centre[1:2]], axis=1) for m in mean_rows]
        apart = jnp.concatenate(apart, axis=0)
        docs = own_ref.shape[0]
        shift = over_rows(*stacked(jnp.concatenate([apart, jnp.zeros_like(apart)], axis=0))) * jnp.float32(docs)
        work[:LANES, :LANES] = unfold(first) + shift[:LANES, :LANES]
        work[:64, LANES:] = first[96:TRIANGLE] + shift[:64, LANES:]
        work[64:LANES, LANES:] = second[96:TRIANGLE] + shift[64:LANES, LANES:]
        work[LANES:, LANES:] = unfold(second) + shift[LANES:, LANES:]
        work[LANES:, :LANES] = jnp.zeros((LANES, LANES), F32)
        mean_at = lax.broadcasted_iota(I32, (8, SKETCH), 0) == 2 * my_x + my_core
        own_shift = jnp.sum(jnp.where(mean_at, apart, 0.0), axis=0, keepdims=True)

        for start in range(0, size, PIVOTS):
            rest = start + PIVOTS
            factor_rows = eliminate(work[start:rest, :], start)
            work[start:rest, :] = factor_rows
            if rest < size:
                left, right = stacked(factor_rows)
                from_col = rest // LANES * LANES
                update = over_rows(left[:, from_col:], right)
                old = work[rest:, :]
                column = lax.broadcasted_iota(I32, old.shape, 1)
                old = jnp.where((column >= start) & (column < rest), 0.0, old)
                work[rest:, :] = old - update[rest - from_col :, :]

        row = lax.broadcasted_iota(I32, (size, size), 0)
        column = lax.broadcasted_iota(I32, (size, size), 1)
        inverse = jnp.where(column <= row, work[...], 0.0)
        own = own_ref[...] + own_shift
        inverse_ref[...] = inverse
        shifted_ref[...] = own
        flipped = by_rows(inverse, own).astype(BF16)
        rows = size // 8
        for x in range(4):
            place = (x - my_x) & 3
            place = jnp.where(place == 2, 0, jnp.where(place == 3, 2, jnp.where(place == 1, 1, 3)))
            for core in range(2):
                piece = flipped[rows * (2 * x + core) : rows * (2 * x + core + 1)]
                bt_ref[place, (my_core + core) & 1] = piece

    fetch.wait()


def basis_call(mine, theirs, own, weighted):
    rows = own.shape[0]
    in_vmem = pl.BlockSpec(memory_space=pltpu.VMEM)
    in_hbm = pl.BlockSpec(memory_space=pltpu.HBM)
    return pl.pallas_call(
        basis_kernel,
        in_specs=[in_vmem] * 3 + [in_hbm],
        out_specs=[in_vmem] * 4,
        out_shape=[
            jax.ShapeDtypeStruct((SKETCH, SKETCH), F32),
            jax.ShapeDtypeStruct((rows, SKETCH), F32),
            jax.ShapeDtypeStruct((4, 2, SKETCH // 8, rows), BF16),
            pltpu.VMEM(weighted.shape, BF16),
        ],
        scratch_shapes=[pltpu.VMEM((SKETCH, SKETCH), F32), pltpu.SemaphoreType.DMA],
        compiler_params=pltpu.CompilerParams(vmem_limit_bytes=VMEM_LIMIT),
        name="basis",
    )(mine, theirs, own, pltpu.with_memory_space_constraint(weighted, pltpu.HBM))


def log_means(mine_ref, theirs_ref, docs):
    tail = TRIANGLE + MEANS
    on_first = lax.axis_index("core") == 0
    low = jnp.where(on_first, mine_ref[tail:], theirs_ref[tail:])
    high = jnp.where(on_first, theirs_ref[tail:], mine_ref[tail:])
    return jnp.concatenate([low, high], axis=0) * (1.0 / docs)


def project_kernel(bt_ref, w_ref, centre_ref, idf_ref, mine_ref, theirs_ref, *out_refs, pieces):
    _, cores, rows, depth = bt_ref.shape
    width = w_ref.shape[1]
    left = bt_ref[:pieces].reshape(pieces * cores * rows, depth)
    sums = jnp.sum(left.astype(F32), axis=1, keepdims=True)
    apart = idf_ref[...] * (centre_ref[...] - log_means(mine_ref, theirs_ref, 8 * depth))
    block = 512
    for at in range(0, width, block):
        product = jnp.dot(left, w_ref[:depth, at : at + block], preferred_element_type=F32)
        row = at // LANES
        shift = jnp.concatenate([apart[row + k : row + k + 1] for k in range(block // LANES)], axis=1)
        product = (product + sums * shift).astype(BF16)
        for k in range(pieces * cores):
            value = product[k * rows : (k + 1) * rows]
            if k >= cores:
                out_refs[cores + k][:, at : at + block] = value
            else:
                begin = at % (width // 2)
                out_refs[2 * (2 * at // width) + k][:, begin : begin + block] = value


def finish_kernel(own_ref, inverse_ref, idf_ref, mine_ref, theirs_ref, q_ref, mean_ref):
    q_ref[...] = by_rows(own_ref[...], inverse_ref[...])
    docs = 8 * own_ref.shape[0]
    mean_ref[...] = idf_ref[...] * (1.0 + log_means(mine_ref, theirs_ref, docs))


def project_call(kernel, outs, operands):
    in_vmem = pl.BlockSpec(memory_space=pltpu.VMEM)
    return pl.pallas_call(
        kernel,
        in_specs=[in_vmem] * len(operands),
        out_specs=[in_vmem] * len(outs),
        out_shape=outs,
        compiler_params=pltpu.CompilerParams(vmem_limit_bytes=24 * 1024 * 1024),
        name="project",
    )(*operands)


def swap(value):
    return lax.ppermute(value, "core", [(0, 1), (1, 0)])


def shift_x(value, by):
    return lax.ppermute(value, "x", [(i, (i + by) % 4) for i in range(4)])


def three_sum(a, b, c):
    return (a.astype(F32) + b.astype(F32) + c.astype(F32)).astype(BF16)


def half_sum(a, b):
    return (a.astype(F32) + b.astype(F32)).astype(BF16)


def body(counts, doc_freq, sketch_seed):
    rows, cols = counts.shape
    terms_axes = ("y", "z")
    parts = lax.axis_size(terms_axes)

    sketch_part, weighted, log_sums, centres, idf = sketch_call(sketch_seed, counts, doc_freq, parts)

    pieces = lax.all_to_all(sketch_part, terms_axes, 0, 0)
    gathered = lax.all_to_all(share_call(pieces), terms_axes, 0, 0)
    payload, own = gram_call(gathered, log_sums, rows)

    mine = payload[0] + swap(payload[1])
    mine = (mine + shift_x(mine, 2)) + (shift_x(mine, 1) + shift_x(mine, 3))
    theirs = swap(mine)
    inverse, own, flipped, weighted = basis_call(mine, theirs, own, weighted)

    half = cols // 2
    narrow, wide = (jax.ShapeDtypeStruct((SKETCH // 8, n), BF16) for n in (half, cols))
    rest = (weighted, centres, idf, mine, theirs)
    ours2a, other2a, ours2b, other2b, ours1, other1, ours3, other3, ours0, other0 = project_call(
        functools.partial(project_kernel, pieces=4), [narrow] * 4 + [wide] * 6, (flipped,) + rest
    )
    relay_up = shift_x(half_sum(ours2a, swap(other2a)), 1)
    relay_down = shift_x(half_sum(ours2b, swap(other2b)), -1)
    theirs1, theirs3 = swap(other1), swap(other3)
    near_up = half_sum(ours1[:, half:], theirs1[:, half:])
    near_down = half_sum(ours3[:, :half], theirs3[:, :half])
    theirs1, theirs3, near_up, near_down = lax.optimization_barrier((theirs1, theirs3, near_up, near_down))
    below_b, above_a = shift_x(near_up, 1), shift_x(near_down, -1)
    below_a = shift_x(three_sum(ours1[:, :half], theirs1[:, :half], relay_up), 1)
    above_b = shift_x(three_sum(ours3[:, half:], theirs3[:, half:], relay_down), -1)
    own, _, _ = lax.optimization_barrier((own, theirs1, theirs3))
    basis, means = project_call(
        finish_kernel,
        [jax.ShapeDtypeStruct(own.shape, F32), jax.ShapeDtypeStruct(idf.shape, F32)],
        (own, inverse, idf, mine, theirs),
    )
    total = ours0.astype(F32) + swap(other0).astype(F32)
    below = jnp.concatenate([below_a, below_b], axis=1).astype(F32)
    above = jnp.concatenate([above_a, above_b], axis=1).astype(F32)
    total = total + below + above
    return (basis, total.astype(BF16), means.reshape(cols))


def solution(mesh):
    split = Mesh(np.array(mesh.devices).reshape(4, 2, 4, 8), ("x", "core", "y", "z"))
    docs, terms = ("x", "core"), ("y", "z")
    return jax.shard_map(
        body,
        mesh=split,
        in_specs=(P(docs, terms), P(terms), P()),
        out_specs=(P(docs, None), P(docs, terms), P(terms)),
        check_vma=False,
    )
```
